1024 devices in a mesh: dp: 64 (over z, core), expert: 16 (over y, x).
Axes of the slice: x: 4, y: 4, z: 32, core: 2. Of those that a mesh axis runs over, the one named last changes fastest.
Arguments:
- grads: bfloat16 [16, 128, 1024, 384], P('expert', None, 'dp'), may hold values from -6 to 6
- counts: int32 [16], P('expert'), may hold values from 1 to 127, as said below
Outputs:
- updates: bfloat16 [16, 128, 1024, 384], P('expert', None, 'dp')
The draws below stay inside these ranges and needn't reach their ends.
Inputs may be any that keep to these rules, and one draw needn't show every extreme that they name: Ranks 2k and 2k+1 form pairs: in each pair one rank owns more than 64 matrices, and the pair's two counts sum to at most 128.
All inputs are finite; a program needn't handle non-finite values.
Results may differ from the reference program's by a relative error of at most 0.0058.
Values may be sent and summed in bfloat16 or wider, within the bound.
A program may use at most 32 MiB of HBM per device.

```python
import math
import jax
import jax.numpy as jnp
from jax import lax

ROWS = 1024
COLS = 384
NS_STEPS = 2
SLOTS = 128
N_EXPERT = 16


def draw_counts(key, part):
    pair_count = N_EXPERT // 2
    key_heavy = jax.random.fold_in(key, 11)
    key_light = jax.random.fold_in(key, 23)
    key_order = jax.random.fold_in(key, 37)
    heavier = jax.random.randint(key_heavy, (pair_count,), SLOTS // 2 + 1, SLOTS)
    pair_ids = jnp.arange(pair_count, dtype=jnp.int32)
    last_pair = pair_ids == pair_count - 1
    heavier = jnp.where(last_pair, SLOTS - 1, heavier)
    spare_room = SLOTS - heavier
    lighter = jax.random.randint(key_light, (pair_count,), 1, spare_room + 1)
    heavy_first = jax.random.randint(key_order, (pair_count,), 0, 2)
    heavy_first = jnp.where(last_pair, 1, heavy_first)
    first_rank = jnp.where(heavy_first == 1, heavier, lighter)
    second_rank = jnp.where(heavy_first == 1, lighter, heavier)
    return jnp.stack([first_rank, second_rank], axis=1).reshape(-1).astype(jnp.int32)


def levels(stream_key, extent, split, low, high):
    gain, own = 1.0, jax.random.fold_in(stream_key, 6)
    for dim, parts in split:
        heights = jnp.exp(jax.random.uniform(jax.random.fold_in(own, dim), (parts,), jnp.float32, low / len(split), high / len(split)))
        gain = gain * jnp.repeat(heights, extent[dim] // parts).reshape([-1 if axis == dim else 1 for axis in range(len(extent))])
    return gain


def scatter_about(stream_key, dims, scale, bound, pieces=(), held_as=jnp.bfloat16):
    values = scale * jax.random.normal(stream_key, dims, jnp.float32)
    if pieces:
        values = values * levels(stream_key, dims, pieces, -0.22, 0.18)
    return jnp.clip(values, -bound, bound).astype(held_as)


def setup_inputs(seed: int = 0) -> dict:
    arg_keys = jax.random.split(jax.random.key(seed), 3)
    grads = scatter_about(arg_keys[0], (N_EXPERT, SLOTS, ROWS, COLS), 1.0, 6.0, ((0, 16), (2, 64)))
    counts = draw_counts(jax.random.fold_in(arg_keys[2], 71), 0)
    return dict(grads=grads, counts=counts)


poly_first = 3.4445
poly_second = -4.775
poly_third = 2.0315

def orthogonalize(matrix):
    values = matrix.astype(jnp.float32)
    frob_norm = jnp.sqrt(jnp.sum(values * values))
    current = (values / (frob_norm + 1e-07)).astype(jnp.bfloat16)
    scale_out = math.sqrt(matrix.shape[0])
    result = jnp.zeros_like(matrix)
    for iteration in range(NS_STEPS):
        gram_matrix = lax.dot_general(current, current, (((0,), (0,)), ((), ())), preferred_element_type=jnp.float32).astype(jnp.bfloat16)
        squared = jnp.dot(gram_matrix, gram_matrix, preferred_element_type=jnp.float32)
        poly_matrix = (poly_second * gram_matrix.astype(jnp.float32) + poly_third * squared).astype(jnp.bfloat16)
        updated = poly_first * current.astype(jnp.float32) + jnp.dot(current, poly_matrix, preferred_element_type=jnp.float32)
        if iteration + 1 < NS_STEPS:
            current = updated.astype(jnp.bfloat16)
        else:
            result = (updated * scale_out).astype(jnp.bfloat16)
    return result

def blank(matrix):
    return jnp.zeros_like(matrix)

def reference(grads, counts):
    flat = grads.reshape(N_EXPERT * SLOTS, ROWS, COLS)
    slot_ids = jnp.arange(SLOTS, dtype=jnp.int32)
    live_flags = (slot_ids[None, :] < counts[:, None]).reshape(-1)

    def handle(item):
        matrix, flag = item
        return lax.cond(flag, orthogonalize, blank, matrix)
    updates = lax.map(handle, (flat, live_flags))
    return updates.reshape(grads.shape)
```

```python
import functools
import math

import jax
import jax.numpy as jnp
from jax import lax
from jax.experimental import pallas as pl
from jax.experimental.pallas import tpu as pltpu
from jax.sharding import PartitionSpec as P

NS_STEPS = 2
GROUPS = 8
CHUNKS = 4

poly_first = 3.4445
poly_second = -4.775
poly_third = 2.0315

MESH = pl.DeviceIdType.MESH


def transposed_dot(a):
    return lax.dot_general(a, a, (((0,), (0,)), ((), ())), preferred_element_type=jnp.float32)


def polynomial(gram):
    squared = jnp.dot(gram, gram, preferred_element_type=jnp.float32)
    return (poly_second * gram.astype(jnp.float32) + poly_third * squared).astype(jnp.bfloat16)


def kernel(
    D, grads, counts, out,
    own, xin, packed, gath, cur, done,
    load_sem, xin_send, xin_recv, z_send, z_recv, self_sem, back_send, back_recv, xout_send, xout_recv,
):
    Z = D // 2
    strip, cols = grads.shape[1], grads.shape[2]
    per_group = D // GROUPS
    per_chunk = D // CHUNKS
    me = lax.axis_index("dp")
    expert = lax.axis_index("expert")
    mate = expert + 1 - 2 * lax.rem(expert, 2)
    z, core = me // 2, lax.rem(me, 2)

    load = pltpu.make_async_copy(grads.at[pl.ds(0, D)], own, load_sem)
    load.start()

    barrier = pltpu.get_barrier_semaphore()

    @pl.loop(1, D)
    def _(k):
        pl.semaphore_signal(
            barrier, inc=1, device_id=(lax.rem(me + k, D), expert), device_id_type=MESH
        )

    pl.semaphore_signal(barrier, inc=1, device_id=(me, mate), device_id_type=MESH)
    pl.semaphore_wait(barrier, D)

    def offset(m):
        return jnp.where(lax.rem(m, 2) == 1, (m + 1) // 2, Z - m // 2)

    def slot_of(i):
        w, m = i // Z, lax.rem(i, Z)
        return lax.rem(z + offset(m), Z) * 2 + w, w, m

    @pl.loop(0, D)
    def _(i):
        j, _, _ = slot_of(i)
        pltpu.make_async_remote_copy(
            src_ref=grads.at[2 * D - 1 - j],
            dst_ref=xin.at[j],
            send_sem=xin_send,
            recv_sem=xin_recv.at[i // per_group],
            device_id=(me, mate),
            device_id_type=MESH,
        ).start()

    load.wait()
    count = counts[0]

    @pl.loop(0, GROUPS)
    def _(g):
        pltpu.make_async_copy(
            xin.at[pl.ds(0, per_group)], xin.at[pl.ds(0, per_group)], xin_recv.at[g]
        ).wait()

        @pl.loop(0, per_group)
        def _(k):
            j, w, m = slot_of(g * per_group + k)
            packed[j] = jnp.where(j < count, own[j], xin[j])

            @pl.when(j != me)
            def _():
                pltpu.make_async_remote_copy(
                    src_ref=packed.at[j],
                    dst_ref=gath.at[2 * m + core],
                    send_sem=z_send,
                    recv_sem=z_recv.at[2 * m // per_chunk],
                    device_id=(j, expert),
                    device_id_type=MESH,
                ).start()

            @pl.when(j == me)
            def _():
                gath[core] = packed[j]

    gram_sum = jnp.zeros((cols, cols), jnp.float32)
    for c in range(CHUNKS):
        n = per_chunk - 1 if c == 0 else per_chunk
        pltpu.make_async_copy(gath.at[pl.ds(0, n)], gath.at[pl.ds(0, n)], z_recv.at[c]).wait()
        part = gath[c * per_chunk : (c + 1) * per_chunk].reshape(per_chunk * strip, cols)
        gram_sum = gram_sum + transposed_dot(part)
    rows_i = lax.broadcasted_iota(jnp.int32, (cols, cols), 0)
    cols_i = lax.broadcasted_iota(jnp.int32, (cols, cols), 1)
    square_sum = jnp.sum(jnp.where(rows_i == cols_i, gram_sum, 0.0), keepdims=True)
    inv = 1.0 / (jnp.sqrt(square_sum) + 1e-07)
    gram = (gram_sum * inv * inv).astype(jnp.bfloat16)
    poly = polynomial(gram)
    gram_sum = jnp.zeros((cols, cols), jnp.float32)
    for c in range(CHUNKS):
        part = gath[c * per_chunk : (c + 1) * per_chunk].reshape(per_chunk * strip, cols)
        part = (part.astype(jnp.float32) * inv).astype(jnp.bfloat16)
        updated = poly_first * part.astype(jnp.float32) + jnp.dot(
            part, poly, preferred_element_type=jnp.float32
        )
        updated = updated.astype(jnp.bfloat16)
        cur[c] = updated
        gram_sum = gram_sum + transposed_dot(updated)
    poly = polynomial(gram_sum.astype(jnp.bfloat16))
    scale_out = math.sqrt(D * strip)

    def back(m, s):
        zs = lax.rem(z + Z - offset(m), Z)
        return pltpu.make_async_remote_copy(
            src_ref=done.at[2 * m + s],
            dst_ref=out.at[me],
            send_sem=back_send,
            recv_sem=back_recv.at[(core * Z + m) // per_group],
            device_id=(zs * 2 + s, expert),
            device_id_type=MESH,
        )

    for c in range(CHUNKS):
        part = cur[c]
        updated = poly_first * part.astype(jnp.float32) + jnp.dot(
            part, poly, preferred_element_type=jnp.float32
        )
        done[c * per_chunk : (c + 1) * per_chunk] = (
            (updated * scale_out).astype(jnp.bfloat16).reshape(per_chunk, strip, cols)
        )

        @pl.loop(0, per_chunk)
        def _(k):
            i = c * per_chunk + k
            m, s = i // 2, lax.rem(i, 2)

            @pl.when(i != core)
            def _():
                back(m, s).start()

        if c == 0:
            pltpu.make_async_copy(done.at[core], out.at[me], self_sem).start()

    pltpu.make_async_copy(done.at[core], out.at[me], self_sem).wait()

    @pl.loop(0, GROUPS)
    def _(g):
        first = g == core * (GROUPS // 2)

        @pl.when(first)
        def _():
            if per_group > 1:
                pltpu.make_async_copy(
                    xin.at[pl.ds(0, per_group - 1)], xin.at[pl.ds(0, per_group - 1)], back_recv.at[g]
                ).wait()

        @pl.when(jnp.logical_not(first))
        def _():
            pltpu.make_async_copy(
                xin.at[pl.ds(0, per_group)], xin.at[pl.ds(0, per_group)], back_recv.at[g]
            ).wait()

        @pl.loop(0, per_group)
        def _(k):
            j, _, _ = slot_of(g * per_group + k)
            pltpu.make_async_remote_copy(
                src_ref=out.at[j],
                dst_ref=out.at[2 * D - 1 - j],
                send_sem=xout_send,
                recv_sem=xout_recv,
                device_id=(me, mate),
                device_id_type=MESH,
            ).start()

    def wait_all(ref, sem):
        pltpu.make_async_copy(ref, ref, sem).wait()

    wait_all(xin, xin_send)
    wait_all(packed.at[pl.ds(0, D - 1)], z_send)
    wait_all(done.at[pl.ds(0, D - 1)], back_send)
    wait_all(out.at[pl.ds(0, D)], xout_send)
    wait_all(out.at[pl.ds(0, D)], xout_recv)


def body(D, grads, counts):
    held = grads[0]
    slots, strip, cols = held.shape
    bf16 = functools.partial(pltpu.VMEM, dtype=jnp.bfloat16)
    dma = pltpu.SemaphoreType.DMA
    moved = pl.pallas_call(
        functools.partial(kernel, D),
        out_shape=jax.ShapeDtypeStruct((slots, strip, cols), jnp.bfloat16),
        in_specs=[pl.BlockSpec(memory_space=pl.ANY), pl.BlockSpec(memory_space=pltpu.SMEM)],
        out_specs=pl.BlockSpec(memory_space=pl.ANY),
        scratch_shapes=[
            bf16((D, strip, cols)),
            bf16((D, strip, cols)),
            bf16((D, strip, cols)),
            bf16((D, strip, cols)),
            bf16((CHUNKS, D * strip // CHUNKS, cols)),
            bf16((D, strip, cols)),
            dma,
            dma,
            dma((GROUPS,)),
            dma,
            dma((CHUNKS,)),
            dma,
            dma,
            dma((GROUPS,)),
            dma,
            dma,
        ],
        compiler_params=pltpu.CompilerParams(
            collective_id=0, has_side_effects=True, vmem_limit_bytes=32 * 1024 * 1024
        ),
    )(held, counts)
    slot_ids = jnp.arange(slots, dtype=jnp.int32)
    result = jnp.where((slot_ids < counts[0])[:, None, None], moved, jnp.zeros_like(moved))
    return result[None]


def solution(mesh):
    placed = (P("expert", None, "dp", None), P("expert"))
    return jax.shard_map(
        functools.partial(body, mesh.shape["dp"]),
        mesh=mesh,
        in_specs=placed,
        out_specs=P("expert", None, "dp", None),
        check_vma=False,
    )
```

```python
import functools
import math

import jax
import jax.numpy as jnp
from jax import lax
from jax.experimental import pallas as pl
from jax.experimental.pallas import tpu as pltpu
from jax.sharding import PartitionSpec as P

GROUPS = 8
PARTS = 16
BLOCK = 128
PRIMARY, SECONDARY = 0, 1

poly_first = 3.4445
poly_second = -4.775
poly_third = 2.0315

MESH = pl.DeviceIdType.MESH


def transposed_dot(a):
    return lax.dot_general(a, a, (((0,), (0,)), ((), ())), preferred_element_type=jnp.float32)


def dot(a, b):
    return jnp.dot(a, b, preferred_element_type=jnp.float32)


def polynomial(gram):
    squared = dot(gram, gram)
    return (poly_second * gram.astype(jnp.float32) + poly_third * squared).astype(jnp.bfloat16)


def gram_after(gram, poly):
    half = dot(poly, gram)
    high = half.astype(jnp.bfloat16)
    low = (half - high.astype(jnp.float32)).astype(jnp.bfloat16)
    whole = dot(high, poly) + dot(low, poly)
    whole = poly_first * poly_first * gram.astype(jnp.float32) + 2 * poly_first * half + whole
    return whole.astype(jnp.bfloat16)


def plain_blocks(cols):
    n = cols // BLOCK
    return [(a, b) for a in range(n) for b in range(a, n) if a != b or a > 1]


def block(a, b):
    return slice(a * BLOCK, (a + 1) * BLOCK), slice(b * BLOCK, (b + 1) * BLOCK)


def pack(gram, trace, blocks, put):
    r = lax.broadcasted_iota(jnp.int32, (BLOCK, BLOCK), 0)
    c = lax.broadcasted_iota(jnp.int32, (BLOCK, BLOCK), 1)
    first, second = gram[block(0, 0)], gram[block(1, 1)]
    put(0, BLOCK, jnp.where(r <= c, first, second))
    for index, at in enumerate(blocks, 1):
        put(index * BLOCK, BLOCK, gram[block(*at)])
    diagonal = jnp.sum(jnp.where(r == c, second, 0.0), axis=0, keepdims=True)
    high = trace.astype(jnp.bfloat16).astype(jnp.float32)
    r = lax.broadcasted_iota(jnp.int32, (16, BLOCK), 0)
    tail = jnp.where(r == 0, high, jnp.where(r == 1, trace - high, diagonal))
    put((len(blocks) + 1) * BLOCK, 16, tail)


def unpack(blocks, get):
    r = lax.broadcasted_iota(jnp.int32, (BLOCK, BLOCK), 0)
    c = lax.broadcasted_iota(jnp.int32, (BLOCK, BLOCK), 1)
    both = get(0, BLOCK)
    turned = both.T
    tail = get((len(blocks) + 1) * BLOCK, 16)
    trace = tail[0:1, 0:1] + tail[1:2, 0:1]
    first = jnp.where(r <= c, both, turned)
    second = jnp.where(r > c, both, jnp.where(r < c, turned, tail[2:3]))
    found = [((0, 0), first), ((1, 1), second)]
    return trace, found + [(at, get(i * BLOCK, BLOCK)) for i, at in enumerate(blocks, 1)]


def kernel(
    D, grads, counts, out,
    own, xin, packed, gath, done, gram_own, gram_out, gram_in, gram_all,
    load_sem, xin_send, xin_recv, z_send, z_recv, self_sem, back_send, back_recv, xout_send, xout_recv,
    gram_send, gram_recv,
):
    Z = D // 2
    span = Z // 4
    reach = 3 * Z // 8
    strip, cols = grads.shape[1], grads.shape[2]
    half = D // 2
    per_group = D // GROUPS
    per_part = D // PARTS
    per_chunk = D // 4
    blocks = plain_blocks(cols)
    me = lax.axis_index("dp")
    expert = lax.axis_index("expert")
    mate = expert + 1 - 2 * lax.rem(expert, 2)
    z, core = me // 2, lax.rem(me, 2)

    load = pltpu.make_async_copy(grads.at[pl.ds(0, D)], own, load_sem)
    load.start()

    barrier = pltpu.get_barrier_semaphore()

    @pl.loop(0, 2 * reach + 1)
    def _(k):
        far = lax.rem(z + Z + reach - k, Z) * 2

        @pl.loop(0, 2)
        def _(s):
            @pl.when(far + s != me)
            def _():
                pl.semaphore_signal(
                    barrier, inc=1, device_id=(far + s, expert), device_id_type=MESH
                )

    pl.semaphore_signal(barrier, inc=1, device_id=(me, mate), device_id_type=MESH)
    pl.semaphore_wait(barrier, 2 * (2 * reach + 1))

    def offset(role, m, s):
        return jnp.where(role == PRIMARY, reach - s - m, 1 - reach - s + m)

    def target_of(w, role, m):
        zt = z + offset(role, m, core) + 2 * Z
        slot = lax.rem(zt - role * span, Z) * 2 + w
        return slot, lax.rem(zt, Z) * 2 + w

    def outward(i):
        w, q = i // Z, lax.rem(i, Z)
        return w, lax.rem(q, 2), q // 2

    def homeward(i):
        w, q = i // Z, lax.rem(i, Z)
        return w, q // (Z // 2), lax.rem(q, Z // 2)

    def cross(g):
        @pl.loop(0, per_group)
        def _(k):
            j, _ = target_of(*outward(g * per_group + k))
            pltpu.make_async_remote_copy(
                src_ref=grads.at[2 * D - 1 - j],
                dst_ref=xin.at[j],
                send_sem=xin_send,
                recv_sem=xin_recv.at[g],
                device_id=(me, mate),
                device_id_type=MESH,
            ).start()

    cross(0)
    cross(1)

    load.wait()
    count = counts[0]

    @pl.loop(0, GROUPS)
    def _(g):
        @pl.when(g < GROUPS - 2)
        def _():
            cross(g + 2)

        pltpu.make_async_copy(
            xin.at[pl.ds(0, per_group)], xin.at[pl.ds(0, per_group)], xin_recv.at[g]
        ).wait()

        @pl.loop(0, per_group)
        def _(k):
            w, role, m = outward(g * per_group + k)
            j, target = target_of(w, role, m)
            packed[j] = jnp.where(j < count, own[j], xin[j])

            @pl.when(target != me)
            def _():
                pltpu.make_async_remote_copy(
                    src_ref=packed.at[j],
                    dst_ref=gath.at[role * half + 2 * m + core],
                    send_sem=z_send,
                    recv_sem=z_recv.at[2 * role + 2 * m // per_chunk],
                    device_id=(target, expert),
                    device_id_type=MESH,
                ).start()

            @pl.when(target == me)
            def _():
                gath[role * half + 2 * m + core] = packed[j]

    def exchange(role):
        zt = lax.rem(z + (span if role == PRIMARY else Z - span), Z)
        return pltpu.make_async_remote_copy(
            src_ref=gram_out.at[role],
            dst_ref=gram_in.at[1 - role],
            send_sem=gram_send.at[role],
            recv_sem=gram_recv.at[1 - role],
            device_id=(zt * 2 + core, expert),
            device_id_type=MESH,
        )

    def rows_of(role, c):
        start = role * half + c * per_chunk
        return gath[start : start + per_chunk].reshape(per_chunk * strip, cols)

    rows_i = lax.broadcasted_iota(jnp.int32, (cols, cols), 0)
    cols_i = lax.broadcasted_iota(jnp.int32, (cols, cols), 1)
    traces = []
    for role in (PRIMARY, SECONDARY):
        gram = jnp.zeros((cols, cols), jnp.float32)
        for c in range(2):
            n = per_chunk - c
            pltpu.make_async_copy(
                gath.at[pl.ds(0, n)], gath.at[pl.ds(0, n)], z_recv.at[2 * role + c]
            ).wait()
            gram = gram + transposed_dot(rows_of(role, c))
        gram_own[role] = gram
        trace = jnp.sum(jnp.where(rows_i == cols_i, gram, 0.0), keepdims=True)

        def put(start, n, values, role=role):
            gram_out[role, start : start + n] = values.astype(jnp.bfloat16)

        pack(gram, trace, blocks, put)
        traces.append(trace)
        exchange(role).start()

    def back(role, m, s):
        zs = lax.rem(z - offset(role, m, s) + 2 * Z, Z)
        slot = lax.rem(z + Z - role * span, Z) * 2 + core
        return zs * 2 + s, pltpu.make_async_remote_copy(
            src_ref=done.at[role * half + 2 * m + s],
            dst_ref=out.at[slot],
            send_sem=back_send,
            recv_sem=back_recv.at[(core * Z + role * (Z // 2) + m) // per_part],
            device_id=(zs * 2 + s, expert),
            device_id_type=MESH,
        )

    def own_m(role):
        return reach - core if role == PRIMARY else reach - 1 + core

    def keep(role):
        m = own_m(role)
        slot = lax.rem(z + Z - role * span, Z) * 2 + core
        return pltpu.make_async_copy(
            done.at[role * half + 2 * m + core], out.at[slot], self_sem.at[role]
        )

    scale_out = math.sqrt(D * strip)
    for role in (PRIMARY, SECONDARY):
        exchange(1 - role).wait_recv()

        def get(start, n, role=role):
            return gram_in[role, start : start + n].astype(jnp.float32)

        trace, others = unpack(blocks, get)
        inv = 1.0 / (jnp.sqrt(traces[role] + trace) + 1e-07)
        for (a, b), other in others:
            whole = (gram_own[(role, *block(a, b))] + other) * inv * inv
            gram_all[block(a, b)] = whole.astype(jnp.bfloat16)
            if a != b:
                gram_all[block(b, a)] = whole.T.astype(jnp.bfloat16)
        gram = gram_all[...]
        poly = polynomial(gram)
        next_poly = polynomial(gram_after(gram, poly))
        for c in range(2):
            part = (rows_of(role, c).astype(jnp.float32) * inv).astype(jnp.bfloat16)
            part = (poly_first * part.astype(jnp.float32) + dot(part, poly)).astype(jnp.bfloat16)
            updated = poly_first * part.astype(jnp.float32) + dot(part, next_poly)
            start = role * half + c * per_chunk
            done[start : start + per_chunk] = (
                (updated * scale_out).astype(jnp.bfloat16).reshape(per_chunk, strip, cols)
            )

            @pl.loop(0, per_chunk)
            def _(k):
                i = c * per_chunk + k
                target, copy = back(role, i // 2, lax.rem(i, 2))

                @pl.when(target != me)
                def _():
                    copy.start()

        keep(role).start()

    keep(PRIMARY).wait()
    keep(SECONDARY).wait()

    own_parts = [(core * Z + role * (Z // 2) + own_m(role)) // per_part for role in (0, 1)]

    @pl.loop(0, PARTS)
    def _(g):
        short = jnp.logical_or(g == own_parts[0], g == own_parts[1])

        def arrived(n):
            if n:
                pltpu.make_async_copy(
                    xin.at[pl.ds(0, n)], xin.at[pl.ds(0, n)], back_recv.at[g]
                ).wait()

        @pl.when(short)
        def _():
            arrived(per_part - 1)

        @pl.when(jnp.logical_not(short))
        def _():
            arrived(per_part)

        @pl.loop(0, per_part)
        def _(k):
            j, _ = target_of(*homeward(g * per_part + k))
            pltpu.make_async_remote_copy(
                src_ref=out.at[j],
                dst_ref=out.at[2 * D - 1 - j],
                send_sem=xout_send,
                recv_sem=xout_recv,
                device_id=(me, mate),
                device_id_type=MESH,
            ).start()

    def wait_all(ref, sem):
        pltpu.make_async_copy(ref, ref, sem).wait()

    wait_all(xin, xin_send)
    wait_all(packed.at[pl.ds(0, D - 2)], z_send)
    exchange(PRIMARY).wait_send()
    exchange(SECONDARY).wait_send()
    wait_all(done.at[pl.ds(0, D - 2)], back_send)
    wait_all(out.at[pl.ds(0, D)], xout_send)
    wait_all(out.at[pl.ds(0, D)], xout_recv)


def body(D, grads, counts):
    held = grads[0]
    slots, strip, cols = held.shape
    bf16 = functools.partial(pltpu.VMEM, dtype=jnp.bfloat16)
    dma = pltpu.SemaphoreType.DMA
    gram_rows = (len(plain_blocks(cols)) + 1) * BLOCK + 16
    moved = pl.pallas_call(
        functools.partial(kernel, D),
        out_shape=jax.ShapeDtypeStruct((slots, strip, cols), jnp.bfloat16),
        in_specs=[pl.BlockSpec(memory_space=pl.ANY), pl.BlockSpec(memory_space=pltpu.SMEM)],
        out_specs=pl.BlockSpec(memory_space=pl.ANY),
        scratch_shapes=[
            bf16((D, strip, cols)),
            bf16((D, strip, cols)),
            bf16((D, strip, cols)),
            bf16((D, strip, cols)),
            bf16((D, strip, cols)),
            pltpu.VMEM((2, cols, cols), jnp.float32),
            bf16((2, gram_rows, BLOCK)),
            bf16((2, gram_rows, BLOCK)),
            bf16((cols, cols)),
            dma,
            dma,
            dma((GROUPS,)),
            dma,
            dma((4,)),
            dma((2,)),
            dma,
            dma((PARTS,)),
            dma,
            dma,
            dma((2,)),
            dma((2,)),
        ],
        compiler_params=pltpu.CompilerParams(
            collective_id=0, has_side_effects=True, vmem_limit_bytes=32 * 1024 * 1024
        ),
    )(held, counts)
    slot_ids = jnp.arange(slots, dtype=jnp.int32)
    result = jnp.where((slot_ids < counts[0])[:, None, None], moved, jnp.zeros_like(moved))
    return result[None]


def solution(mesh):
    placed = (P("expert", None, "dp", None), P("expert"))
    return jax.shard_map(
        functools.partial(body, mesh.shape["dp"]),
        mesh=mesh,
        in_specs=placed,
        out_specs=P("expert", None, "dp", None),
        check_vma=False,
    )
```

```python
import functools
import math

import jax
import jax.numpy as jnp
from jax import lax
from jax.experimental import pallas as pl
from jax.experimental.pallas import tpu as pltpu
from jax.sharding import PartitionSpec as P

GROUPS = 8
PARTS = 16
BLOCK = 128
LATER = (15,)
PRIMARY, SECONDARY = 0, 1

poly_first = 3.4445
poly_second = -4.775
poly_third = 2.0315

MESH = pl.DeviceIdType.MESH


def transposed_dot(a):
    return lax.dot_general(a, a, (((0,), (0,)), ((), ())), preferred_element_type=jnp.float32)


def dot(a, b):
    return jnp.dot(a, b, preferred_element_type=jnp.float32)


def polynomial(gram):
    squared = dot(gram, gram)
    return (poly_second * gram.astype(jnp.float32) + poly_third * squared).astype(jnp.bfloat16)


def gram_after(gram, poly):
    half = dot(poly, gram)
    high = half.astype(jnp.bfloat16)
    low = (half - high.astype(jnp.float32)).astype(jnp.bfloat16)
    whole = dot(high, poly) + dot(low, poly)
    whole = poly_first * poly_first * gram.astype(jnp.float32) + 2 * poly_first * half + whole
    return whole.astype(jnp.bfloat16)


def plain_blocks(cols):
    n = cols // BLOCK
    return [(a, b) for a in range(n) for b in range(a, n) if a != b or a > 1]


def block(a, b):
    return slice(a * BLOCK, (a + 1) * BLOCK), slice(b * BLOCK, (b + 1) * BLOCK)


def pack(gram, trace, blocks, put):
    r = lax.broadcasted_iota(jnp.int32, (BLOCK, BLOCK), 0)
    c = lax.broadcasted_iota(jnp.int32, (BLOCK, BLOCK), 1)
    first, second = gram[block(0, 0)], gram[block(1, 1)]
    put(0, BLOCK, jnp.where(r <= c, first, second))
    for index, at in enumerate(blocks, 1):
        put(index * BLOCK, BLOCK, gram[block(*at)])
    diagonal = jnp.sum(jnp.where(r == c, second, 0.0), axis=0, keepdims=True)
    high = trace.astype(jnp.bfloat16).astype(jnp.float32)
    r = lax.broadcasted_iota(jnp.int32, (16, BLOCK), 0)
    tail = jnp.where(r == 0, high, jnp.where(r == 1, trace - high, diagonal))
    put((len(blocks) + 1) * BLOCK, 16, tail)


def unpack(blocks, get):
    r = lax.broadcasted_iota(jnp.int32, (BLOCK, BLOCK), 0)
    c = lax.broadcasted_iota(jnp.int32, (BLOCK, BLOCK), 1)
    both = get(0, BLOCK)
    turned = both.T
    tail = get((len(blocks) + 1) * BLOCK, 16)
    trace = tail[0:1, 0:1] + tail[1:2, 0:1]
    first = jnp.where(r <= c, both, turned)
    second = jnp.where(r > c, both, jnp.where(r < c, turned, tail[2:3]))
    found = [((0, 0), first), ((1, 1), second)]
    return trace, found + [(at, get(i * BLOCK, BLOCK)) for i, at in enumerate(blocks, 1)]


def kernel(
    D, grads, counts, out,
    own, xin, packed, gath, done, gram_own, gram_out, gram_in, gram_all,
    load_sem, xin_send, xin_recv, z_send, z_recv, self_sem, back_send, back_recv, xout_send, xout_recv,
    gram_send, gram_recv,
):
    Z = D // 2
    span = Z // 4
    reach = 3 * Z // 8
    strip, cols = grads.shape[1], grads.shape[2]
    half = D // 2
    per_group = D // GROUPS
    per_part = D // PARTS
    per_chunk = D // 4
    blocks = plain_blocks(cols)
    me = lax.axis_index("dp")
    expert = lax.axis_index("expert")
    mate = expert + 1 - 2 * lax.rem(expert, 2)
    z, core = me // 2, lax.rem(me, 2)

    load = pltpu.make_async_copy(grads.at[pl.ds(0, D)], own, load_sem)
    load.start()

    barrier = pltpu.get_barrier_semaphore()

    @pl.loop(0, 2 * reach + 1)
    def _(k):
        far = lax.rem(z + Z + reach - k, Z) * 2

        @pl.loop(0, 2)
        def _(s):
            @pl.when(far + s != me)
            def _():
                pl.semaphore_signal(
                    barrier, inc=1, device_id=(far + s, expert), device_id_type=MESH
                )

    pl.semaphore_signal(barrier, inc=1, device_id=(me, mate), device_id_type=MESH)
    pl.semaphore_wait(barrier, 2 * (2 * reach + 1))

    def offset(role, m, s):
        return jnp.where(role == PRIMARY, reach - s - m, 1 - reach - s + m)

    def target_of(w, role, m):
        zt = z + offset(role, m, core) + 2 * Z
        slot = lax.rem(zt - role * span, Z) * 2 + w
        return slot, lax.rem(zt, Z) * 2 + w

    def outward(i):
        w, q = i // Z, lax.rem(i, Z)
        return w, lax.rem(q, 2), q // 2

    def turn_of(zj, w):
        return lax.rem(zj // span + w, 2)

    def homeward(i):
        turn, w, q = i // Z, lax.rem(i // (Z // 2), 2), lax.rem(i, Z // 2)
        zj = span * (2 * (q // span) + lax.rem(turn + w, 2)) + lax.rem(q, span)
        return 2 * zj + w

    def part_of(slot):
        zj, w = slot // 2, lax.rem(slot, 2)
        q = zj // (2 * span) * span + lax.rem(zj, span)
        return (turn_of(zj, w) * Z + w * (Z // 2) + q) // per_part

    def cross(g):
        @pl.loop(0, per_group)
        def _(k):
            j, _ = target_of(*outward(g * per_group + k))
            pltpu.make_async_remote_copy(
                src_ref=grads.at[2 * D - 1 - j],
                dst_ref=xin.at[j],
                send_sem=xin_send,
                recv_sem=xin_recv.at[g],
                device_id=(me, mate),
                device_id_type=MESH,
            ).start()

    cross(0)
    cross(1)

    load.wait()
    count = counts[0]

    @pl.loop(0, GROUPS)
    def _(g):
        @pl.when(g < GROUPS - 2)
        def _():
            cross(g + 2)

        pltpu.make_async_copy(
            xin.at[pl.ds(0, per_group)], xin.at[pl.ds(0, per_group)], xin_recv.at[g]
        ).wait()

        @pl.loop(0, per_group)
        def _(k):
            w, role, m = outward(g * per_group + k)
            j, target = target_of(w, role, m)
            packed[j] = jnp.where(j < count, own[j], xin[j])

            @pl.when(target != me)
            def _():
                pltpu.make_async_remote_copy(
                    src_ref=packed.at[j],
                    dst_ref=gath.at[role * half + 2 * m + core],
                    send_sem=z_send,
                    recv_sem=z_recv.at[2 * role + 2 * m // per_chunk],
                    device_id=(target, expert),
                    device_id_type=MESH,
                ).start()

            @pl.when(target == me)
            def _():
                gath[role * half + 2 * m + core] = packed[j]

    roles = [lax.rem(turn + turn_of(z, core), 2) for turn in (0, 1)]

    def exchange(turn):
        zt = lax.rem(z + jnp.where(roles[turn] == PRIMARY, span, Z - span), Z)
        return pltpu.make_async_remote_copy(
            src_ref=gram_out.at[turn],
            dst_ref=gram_in.at[turn],
            send_sem=gram_send.at[turn],
            recv_sem=gram_recv.at[turn],
            device_id=(zt * 2 + core, expert),
            device_id_type=MESH,
        )

    def rows_of(role, c):
        start = role * half + c * per_chunk
        return gath[pl.ds(start, per_chunk)].reshape(per_chunk * strip, cols)

    rows_i = lax.broadcasted_iota(jnp.int32, (cols, cols), 0)
    cols_i = lax.broadcasted_iota(jnp.int32, (cols, cols), 1)
    traces = []
    for turn, role in enumerate(roles):
        gram = jnp.zeros((cols, cols), jnp.float32)
        for c in range(2):
            n = per_chunk - c
            pltpu.make_async_copy(
                gath.at[pl.ds(0, n)], gath.at[pl.ds(0, n)], z_recv.at[2 * role + c]
            ).wait()
            gram = gram + transposed_dot(rows_of(role, c))
        gram_own[turn] = gram
        trace = jnp.sum(jnp.where(rows_i == cols_i, gram, 0.0), keepdims=True)

        def put(start, n, values, turn=turn):
            gram_out[turn, start : start + n] = values.astype(jnp.bfloat16)

        pack(gram, trace, blocks, put)
        traces.append(trace)
        exchange(turn).start()

    def slot_in(role):
        return lax.rem(z + Z - role * span, Z) * 2 + core

    def back(role, m, s):
        zs = lax.rem(z - offset(role, m, s) + 2 * Z, Z)
        return zs, pltpu.make_async_remote_copy(
            src_ref=done.at[role * half + 2 * m + s],
            dst_ref=out.at[slot_in(role)],
            send_sem=back_send,
            recv_sem=back_recv.at[part_of(slot_in(role))],
            device_id=(zs * 2 + s, expert),
            device_id_type=MESH,
        )

    def keep(turn):
        role = roles[turn]
        m = jnp.where(role == PRIMARY, reach - core, reach - 1 + core)
        return pltpu.make_async_copy(
            done.at[role * half + 2 * m + core], out.at[slot_in(role)], self_sem.at[turn]
        )

    scale_out = math.sqrt(D * strip)
    for turn, role in enumerate(roles):
        exchange(turn).wait_recv()

        def get(start, n, turn=turn):
            return gram_in[turn, start : start + n].astype(jnp.float32)

        trace, others = unpack(blocks, get)
        inv = 1.0 / (jnp.sqrt(traces[turn] + trace) + 1e-07)
        for (a, b), other in others:
            whole = (gram_own[(turn, *block(a, b))] + other) * inv * inv
            gram_all[block(a, b)] = whole.astype(jnp.bfloat16)
            if a != b:
                gram_all[block(b, a)] = whole.T.astype(jnp.bfloat16)
        gram = gram_all[...]
        poly = polynomial(gram)
        next_poly = polynomial(gram_after(gram, poly))
        for c in range(2):
            part = (rows_of(role, c).astype(jnp.float32) * inv).astype(jnp.bfloat16)
            part = (poly_first * part.astype(jnp.float32) + dot(part, poly)).astype(jnp.bfloat16)
            updated = poly_first * part.astype(jnp.float32) + dot(part, next_poly)
            start = role * half + c * per_chunk
            done[pl.ds(start, per_chunk)] = (
                (updated * scale_out).astype(jnp.bfloat16).reshape(per_chunk, strip, cols)
            )

        @pl.loop(0, (len(LATER) + 1) * half)
        def _(i):
            s = lax.rem(i, 2)
            zs, copy = back(role, lax.rem(i // 2, Z // 2), s)
            rank = sum((zs >= Z * n // 32).astype(jnp.int32) for n in LATER)

            @pl.when(jnp.logical_and(zs * 2 + s != me, rank == i // half))
            def _():
                copy.start()

        keep(turn).start()

    keep(0).wait()
    keep(1).wait()

    own_parts = [part_of(slot_in(role)) for role in roles]

    @pl.loop(0, PARTS)
    def _(g):
        kept = (g == own_parts[0]).astype(jnp.int32) + (g == own_parts[1]).astype(jnp.int32)

        def arrived(n):
            if n:
                pltpu.make_async_copy(
                    xin.at[pl.ds(0, n)], xin.at[pl.ds(0, n)], back_recv.at[g]
                ).wait()

        @pl.when(kept == 1)
        def _():
            arrived(per_part - 1)

        @pl.when(kept == 0)
        def _():
            arrived(per_part)

        @pl.loop(0, per_part)
        def _(k):
            j = homeward(g * per_part + k)
            pltpu.make_async_remote_copy(
                src_ref=out.at[j],
                dst_ref=out.at[2 * D - 1 - j],
                send_sem=xout_send,
                recv_sem=xout_recv,
                device_id=(me, mate),
                device_id_type=MESH,
            ).start()

    def wait_all(ref, sem):
        pltpu.make_async_copy(ref, ref, sem).wait()

    wait_all(xin, xin_send)
    wait_all(packed.at[pl.ds(0, D - 2)], z_send)
    exchange(0).wait_send()
    exchange(1).wait_send()
    wait_all(done.at[pl.ds(0, D - 2)], back_send)
    wait_all(out.at[pl.ds(0, D)], xout_send)
    wait_all(out.at[pl.ds(0, D)], xout_recv)


def body(D, grads, counts):
    held = grads[0]
    slots, strip, cols = held.shape
    bf16 = functools.partial(pltpu.VMEM, dtype=jnp.bfloat16)
    dma = pltpu.SemaphoreType.DMA
    gram_rows = (len(plain_blocks(cols)) + 1) * BLOCK + 16
    moved = pl.pallas_call(
        functools.partial(kernel, D),
        out_shape=jax.ShapeDtypeStruct((slots, strip, cols), jnp.bfloat16),
        in_specs=[pl.BlockSpec(memory_space=pltpu.HBM), pl.BlockSpec(memory_space=pltpu.SMEM)],
        out_specs=pl.BlockSpec(memory_space=pl.ANY),
        scratch_shapes=[
            bf16((D, strip, cols)),
            bf16((D, strip, cols)),
            bf16((D, strip, cols)),
            bf16((D, strip, cols)),
            bf16((D, strip, cols)),
            pltpu.VMEM((2, cols, cols), jnp.float32),
            bf16((2, gram_rows, BLOCK)),
            bf16((2, gram_rows, BLOCK)),
            bf16((cols, cols)),
            dma,
            dma,
            dma((GROUPS,)),
            dma,
            dma((4,)),
            dma((2,)),
            dma,
            dma((PARTS,)),
            dma,
            dma,
            dma((2,)),
            dma((2,)),
        ],
        compiler_params=pltpu.CompilerParams(
            collective_id=0, has_side_effects=True, vmem_limit_bytes=62 * 1024 * 1024
        ),
    )(held, counts)
    slot_ids = jnp.arange(slots, dtype=jnp.int32)
    result = jnp.where((slot_ids < counts[0])[:, None, None], moved, jnp.zeros_like(moved))
    return result[None]


def solution(mesh):
    placed = (P("expert", None, "dp", None), P("expert"))
    return jax.shard_map(
        functools.partial(body, mesh.shape["dp"]),
        mesh=mesh,
        in_specs=placed,
        out_specs=P("expert", None, "dp", None),
        check_vma=False,
    )
```

```python
import functools
import math

import jax
import jax.numpy as jnp
from jax import lax
from jax.experimental import pallas as pl
from jax.experimental.pallas import tpu as pltpu
from jax.sharding import PartitionSpec as P

GROUPS = 8
PARTS = 16
BLOCK = 128
LATER = (15,)
PRIMARY, SECONDARY = 0, 1

poly_first = 3.4445
poly_second = -4.775
poly_third = 2.0315

MESH = pl.DeviceIdType.MESH


def transposed_dot(a):
    return lax.dot_general(a, a, (((0,), (0,)), ((), ())), preferred_element_type=jnp.float32)


def dot(a, b):
    return jnp.dot(a, b, preferred_element_type=jnp.float32)


def polynomial(gram):
    squared = dot(gram, gram)
    return (poly_second * gram.astype(jnp.float32) + poly_third * squared).astype(jnp.bfloat16)


def gram_after(gram, poly):
    half = dot(poly, gram)
    high = half.astype(jnp.bfloat16)
    low = (half - high.astype(jnp.float32)).astype(jnp.bfloat16)
    whole = dot(high, poly) + dot(low, poly)
    whole = poly_first * poly_first * gram.astype(jnp.float32) + 2 * poly_first * half + whole
    return whole.astype(jnp.bfloat16)


HALF = BLOCK // 2
WHOLE = [(0, 1), (0, 2), (1, 2)]
LAST_AT = (1 + len(WHOLE)) * BLOCK
TAIL_AT = LAST_AT + HALF
GRAM_ROWS = TAIL_AT + 16


def block(a, b):
    return slice(a * BLOCK, (a + 1) * BLOCK), slice(b * BLOCK, (b + 1) * BLOCK)


def iotas(rows):
    return [lax.broadcasted_iota(jnp.int32, (rows, BLOCK), axis) for axis in (0, 1)]


def pack(gram, trace, square, put):
    r, c = iotas(BLOCK)
    first, second, third = gram[block(0, 0)], gram[block(1, 1)], gram[block(2, 2)]
    put(0, BLOCK, jnp.where(r <= c, first, second))
    for index, at in enumerate(WHOLE, 1):
        put(index * BLOCK, BLOCK, gram[block(*at)])
    diagonals = [jnp.sum(jnp.where(r == c, d, 0.0), axis=0, keepdims=True) for d in (second, third)]
    square[:HALF] = third[HALF:]
    square[HALF:] = third[:HALF]
    moved = square[...].T[HALF:]
    r, c = iotas(HALF)
    put(LAST_AT, HALF, jnp.where(r <= c, third[:HALF], moved))
    high = trace.astype(jnp.bfloat16).astype(jnp.float32)
    r, _ = iotas(16)
    tail = jnp.where(r == 2, diagonals[0], diagonals[1])
    put(TAIL_AT, 16, jnp.where(r == 0, high, jnp.where(r == 1, trace - high, tail)))


def unpack(square, get):
    r, c = iotas(BLOCK)
    both = get(0, BLOCK)
    turned = both.T
    tail = get(TAIL_AT, 16)
    trace = tail[0:1, 0:1] + tail[1:2, 0:1]
    first = jnp.where(r <= c, both, turned)
    second = jnp.where(r > c, both, jnp.where(r < c, turned, tail[2:3]))
    mixed = get(LAST_AT, HALF)
    zeros = jnp.zeros((HALF, BLOCK), jnp.float32)
    square[:HALF] = mixed
    square[HALF:] = zeros
    turned = square[...].T
    square[:HALF] = zeros
    square[HALF:] = mixed
    above = square[...].T[:HALF]
    square[HALF:] = turned[:HALF]
    below = square[...].T[:HALF]
    r, c = iotas(HALF)
    top = jnp.where(r <= c, mixed, turned[:HALF])
    d = jnp.where(r > c - HALF, below, jnp.where(r < c - HALF, above, tail[3:4]))
    square[:HALF] = top
    square[HALF:] = jnp.where(c < HALF, turned[HALF:], d)
    found = [((0, 0), first), ((1, 1), second), ((2, 2), square[...])]
    return trace, found + [(at, get(i * BLOCK, BLOCK)) for i, at in enumerate(WHOLE, 1)]


def kernel(
    D, grads, counts, out,
    own, xin, packed, gath, done, gram_own, gram_out, gram_in, gram_all, square,
    load_sem, xin_send, xin_recv, z_send, z_recv, self_sem, back_send, back_recv, xout_send, xout_recv,
    gram_send, gram_recv,
):
    Z = D // 2
    span = Z // 4
    reach = 3 * Z // 8
    strip, cols = grads.shape[1], grads.shape[2]
    half = D // 2
    per_group = D // GROUPS
    per_part = D // PARTS
    per_chunk = D // 4
    me = lax.axis_index("dp")
    expert = lax.axis_index("expert")
    mate = expert + 1 - 2 * lax.rem(expert, 2)
    z, core = me // 2, lax.rem(me, 2)

    load = pltpu.make_async_copy(grads.at[pl.ds(0, D)], own, load_sem)
    load.start()

    barrier = pltpu.get_barrier_semaphore()

    @pl.loop(0, 2 * reach + 1)
    def _(k):
        far = lax.rem(z + Z + reach - k, Z) * 2

        @pl.loop(0, 2)
        def _(s):
            @pl.when(far + s != me)
            def _():
                pl.semaphore_signal(
                    barrier, inc=1, device_id=(far + s, expert), device_id_type=MESH
                )

    pl.semaphore_signal(barrier, inc=1, device_id=(me, mate), device_id_type=MESH)
    pl.semaphore_wait(barrier, 2 * (2 * reach + 1))

    def offset(role, m, s):
        return jnp.where(role == PRIMARY, reach - s - m, 1 - reach - s + m)

    def target_of(w, role, m):
        zt = z + offset(role, m, core) + 2 * Z
        slot = lax.rem(zt - role * span, Z) * 2 + w
        return slot, lax.rem(zt, Z) * 2 + w

    def outward(i):
        w, q = i // Z, lax.rem(i, Z)
        return w, lax.rem(q, 2), q // 2

    def turn_of(zj, w):
        return lax.rem(zj // span + w, 2)

    def homeward(i):
        turn, w, q = i // Z, lax.rem(i // (Z // 2), 2), lax.rem(i, Z // 2)
        zj = span * (2 * (q // span) + lax.rem(turn + w, 2)) + lax.rem(q, span)
        return 2 * zj + w

    def part_of(slot):
        zj, w = slot // 2, lax.rem(slot, 2)
        q = zj // (2 * span) * span + lax.rem(zj, span)
        return (turn_of(zj, w) * Z + w * (Z // 2) + q) // per_part

    def cross(g):
        @pl.loop(0, per_group)
        def _(k):
            j, _ = target_of(*outward(g * per_group + k))
            pltpu.make_async_remote_copy(
                src_ref=grads.at[2 * D - 1 - j],
                dst_ref=xin.at[j],
                send_sem=xin_send,
                recv_sem=xin_recv.at[g],
                device_id=(me, mate),
                device_id_type=MESH,
            ).start()

    cross(0)
    cross(1)

    load.wait()
    count = counts[0]

    @pl.loop(0, GROUPS)
    def _(g):
        @pl.when(g < GROUPS - 2)
        def _():
            cross(g + 2)

        pltpu.make_async_copy(
            xin.at[pl.ds(0, per_group)], xin.at[pl.ds(0, per_group)], xin_recv.at[g]
        ).wait()

        @pl.loop(0, per_group)
        def _(k):
            w, role, m = outward(g * per_group + k)
            j, target = target_of(w, role, m)
            packed[j] = jnp.where(j < count, own[j], xin[j])

            @pl.when(target != me)
            def _():
                pltpu.make_async_remote_copy(
                    src_ref=packed.at[j],
                    dst_ref=gath.at[role * half + 2 * m + core],
                    send_sem=z_send,
                    recv_sem=z_recv.at[2 * role + 2 * m // per_chunk],
                    device_id=(target, expert),
                    device_id_type=MESH,
                ).start()

            @pl.when(target == me)
            def _():
                gath[role * half + 2 * m + core] = packed[j]

    roles = [lax.rem(turn + turn_of(z, core), 2) for turn in (0, 1)]

    def exchange(turn):
        zt = lax.rem(z + jnp.where(roles[turn] == PRIMARY, span, Z - span), Z)
        return pltpu.make_async_remote_copy(
            src_ref=gram_out.at[turn],
            dst_ref=gram_in.at[turn],
            send_sem=gram_send.at[turn],
            recv_sem=gram_recv.at[turn],
            device_id=(zt * 2 + core, expert),
            device_id_type=MESH,
        )

    def rows_of(role, c):
        start = role * half + c * per_chunk
        return gath[pl.ds(start, per_chunk)].reshape(per_chunk * strip, cols)

    rows_i = lax.broadcasted_iota(jnp.int32, (cols, cols), 0)
    cols_i = lax.broadcasted_iota(jnp.int32, (cols, cols), 1)
    traces = []
    for turn, role in enumerate(roles):
        gram = jnp.zeros((cols, cols), jnp.float32)
        for c in range(2):
            n = per_chunk - c
            pltpu.make_async_copy(
                gath.at[pl.ds(0, n)], gath.at[pl.ds(0, n)], z_recv.at[2 * role + c]
            ).wait()
            gram = gram + transposed_dot(rows_of(role, c))
        gram_own[turn] = gram
        trace = jnp.sum(jnp.where(rows_i == cols_i, gram, 0.0), keepdims=True)

        def put(start, n, values, turn=turn):
            gram_out[turn, start : start + n] = values.astype(jnp.bfloat16)

        pack(gram, trace, square, put)
        traces.append(trace)
        exchange(turn).start()

    def slot_in(role):
        return lax.rem(z + Z - role * span, Z) * 2 + core

    def back(role, m, s):
        zs = lax.rem(z - offset(role, m, s) + 2 * Z, Z)
        return zs, pltpu.make_async_remote_copy(
            src_ref=done.at[role * half + 2 * m + s],
            dst_ref=out.at[slot_in(role)],
            send_sem=back_send,
            recv_sem=back_recv.at[part_of(slot_in(role))],
            device_id=(zs * 2 + s, expert),
            device_id_type=MESH,
        )

    def keep(turn):
        role = roles[turn]
        m = jnp.where(role == PRIMARY, reach - core, reach - 1 + core)
        return pltpu.make_async_copy(
            done.at[role * half + 2 * m + core], out.at[slot_in(role)], self_sem.at[turn]
        )

    scale_out = math.sqrt(D * strip)
    for turn, role in enumerate(roles):
        exchange(turn).wait_recv()

        def get(start, n, turn=turn):
            return gram_in[turn, start : start + n].astype(jnp.float32)

        trace, others = unpack(square, get)
        inv = 1.0 / (jnp.sqrt(traces[turn] + trace) + 1e-07)
        for (a, b), other in others:
            whole = (gram_own[(turn, *block(a, b))] + other) * inv * inv
            gram_all[block(a, b)] = whole.astype(jnp.bfloat16)
            if a != b:
                gram_all[block(b, a)] = whole.T.astype(jnp.bfloat16)
        gram = gram_all[...]
        poly = polynomial(gram)
        next_poly = polynomial(gram_after(gram, poly))
        for c in range(2):
            part = (rows_of(role, c).astype(jnp.float32) * inv).astype(jnp.bfloat16)
            part = (poly_first * part.astype(jnp.float32) + dot(part, poly)).astype(jnp.bfloat16)
            updated = poly_first * part.astype(jnp.float32) + dot(part, next_poly)
            start = role * half + c * per_chunk
            done[pl.ds(start, per_chunk)] = (
                (updated * scale_out).astype(jnp.bfloat16).reshape(per_chunk, strip, cols)
            )

        @pl.loop(0, (len(LATER) + 1) * half)
        def _(i):
            s = lax.rem(i, 2)
            zs, copy = back(role, lax.rem(i // 2, Z // 2), s)
            rank = sum((zs >= Z * n // 32).astype(jnp.int32) for n in LATER)

            @pl.when(jnp.logical_and(zs * 2 + s != me, rank == i // half))
            def _():
                copy.start()

        keep(turn).start()

    keep(0).wait()
    keep(1).wait()

    own_parts = [part_of(slot_in(role)) for role in roles]

    @pl.loop(0, PARTS)
    def _(g):
        kept = (g == own_parts[0]).astype(jnp.int32) + (g == own_parts[1]).astype(jnp.int32)

        def arrived(n):
            if n:
                pltpu.make_async_copy(
                    xin.at[pl.ds(0, n)], xin.at[pl.ds(0, n)], back_recv.at[g]
                ).wait()

        @pl.when(kept == 1)
        def _():
            arrived(per_part - 1)

        @pl.when(kept == 0)
        def _():
            arrived(per_part)

        @pl.loop(0, per_part)
        def _(k):
            j = homeward(g * per_part + k)
            pltpu.make_async_remote_copy(
                src_ref=out.at[j],
                dst_ref=out.at[2 * D - 1 - j],
                send_sem=xout_send,
                recv_sem=xout_recv,
                device_id=(me, mate),
                device_id_type=MESH,
            ).start()

    def wait_all(ref, sem):
        pltpu.make_async_copy(ref, ref, sem).wait()

    wait_all(xin, xin_send)
    wait_all(packed.at[pl.ds(0, D - 2)], z_send)
    exchange(0).wait_send()
    exchange(1).wait_send()
    wait_all(done.at[pl.ds(0, D - 2)], back_send)
    wait_all(out.at[pl.ds(0, D)], xout_send)
    wait_all(out.at[pl.ds(0, D)], xout_recv)


def body(D, grads, counts):
    held = grads[0]
    slots, strip, cols = held.shape
    bf16 = functools.partial(pltpu.VMEM, dtype=jnp.bfloat16)
    dma = pltpu.SemaphoreType.DMA
    moved = pl.pallas_call(
        functools.partial(kernel, D),
        out_shape=jax.ShapeDtypeStruct((slots, strip, cols), jnp.bfloat16),
        in_specs=[pl.BlockSpec(memory_space=pltpu.HBM), pl.BlockSpec(memory_space=pltpu.SMEM)],
        out_specs=pl.BlockSpec(memory_space=pl.ANY),
        scratch_shapes=[
            bf16((D, strip, cols)),
            bf16((D, strip, cols)),
            bf16((D, strip, cols)),
            bf16((D, strip, cols)),
            bf16((D, strip, cols)),
            pltpu.VMEM((2, cols, cols), jnp.float32),
            bf16((2, GRAM_ROWS, BLOCK)),
            bf16((2, GRAM_ROWS, BLOCK)),
            bf16((cols, cols)),
            pltpu.VMEM((BLOCK, BLOCK), jnp.float32),
            dma,
            dma,
            dma((GROUPS,)),
            dma,
            dma((4,)),
            dma((2,)),
            dma,
            dma((PARTS,)),
            dma,
            dma,
            dma((2,)),
            dma((2,)),
        ],
        compiler_params=pltpu.CompilerParams(
            collective_id=0, has_side_effects=True, vmem_limit_bytes=62 * 1024 * 1024
        ),
    )(held, counts)
    slot_ids = jnp.arange(slots, dtype=jnp.int32)
    result = jnp.where((slot_ids < counts[0])[:, None, None], moved, jnp.zeros_like(moved))
    return result[None]


def solution(mesh):
    placed = (P("expert", None, "dp", None), P("expert"))
    return jax.shard_map(
        functools.partial(body, mesh.shape["dp"]),
        mesh=mesh,
        in_specs=placed,
        out_specs=P("expert", None, "dp", None),
        check_vma=False,
    )
```

```python
import functools
import math

import jax
import jax.numpy as jnp
from jax import lax
from jax.experimental import pallas as pl
from jax.experimental.pallas import tpu as pltpu
from jax.sharding import PartitionSpec as P

GROUPS = 8
PARTS = 16
BLOCK = 128
LATER = (18,)
PRIMARY, SECONDARY = 0, 1

poly_first = 3.4445
poly_second = -4.775
poly_third = 2.0315

MESH = pl.DeviceIdType.MESH


def transposed_dot(a):
    return lax.dot_general(a, a, (((0,), (0,)), ((), ())), preferred_element_type=jnp.float32)


def dot(a, b):
    return jnp.dot(a, b, preferred_element_type=jnp.float32)


def polynomial(gram):
    squared = dot(gram, gram)
    return (poly_second * gram.astype(jnp.float32) + poly_third * squared).astype(jnp.bfloat16)


def gram_after(gram, poly):
    half = dot(poly, gram)
    high = half.astype(jnp.bfloat16)
    low = (half - high.astype(jnp.float32)).astype(jnp.bfloat16)
    whole = dot(high, poly) + dot(low, poly)
    whole = poly_first * poly_first * gram.astype(jnp.float32) + 2 * poly_first * half + whole
    return whole.astype(jnp.bfloat16)


HALF = BLOCK // 2
WHOLE = [(0, 1), (0, 2), (1, 2)]
LAST_AT = (1 + len(WHOLE)) * BLOCK
TAIL_AT = LAST_AT + HALF
GRAM_ROWS = TAIL_AT + 16


def block(a, b):
    return slice(a * BLOCK, (a + 1) * BLOCK), slice(b * BLOCK, (b + 1) * BLOCK)


def iotas(rows):
    return [lax.broadcasted_iota(jnp.int32, (rows, BLOCK), axis) for axis in (0, 1)]


def pack(gram, trace, square, put):
    r, c = iotas(BLOCK)
    first, second, third = gram[block(0, 0)], gram[block(1, 1)], gram[block(2, 2)]
    put(0, BLOCK, jnp.where(r <= c, first, second))
    for index, at in enumerate(WHOLE, 1):
        put(index * BLOCK, BLOCK, gram[block(*at)])
    diagonals = [jnp.sum(jnp.where(r == c, d, 0.0), axis=0, keepdims=True) for d in (second, third)]
    square[:HALF] = third[HALF:]
    square[HALF:] = third[:HALF]
    moved = square[...].T[HALF:]
    r, c = iotas(HALF)
    put(LAST_AT, HALF, jnp.where(r <= c, third[:HALF], moved))
    high = trace.astype(jnp.bfloat16).astype(jnp.float32)
    r, _ = iotas(16)
    tail = jnp.where(r == 2, diagonals[0], diagonals[1])
    put(TAIL_AT, 16, jnp.where(r == 0, high, jnp.where(r == 1, trace - high, tail)))


def unpack(square, get):
    r, c = iotas(BLOCK)
    both = get(0, BLOCK)
    turned = both.T
    tail = get(TAIL_AT, 16)
    trace = tail[0:1, 0:1] + tail[1:2, 0:1]
    first = jnp.where(r <= c, both, turned)
    second = jnp.where(r > c, both, jnp.where(r < c, turned, tail[2:3]))
    mixed = get(LAST_AT, HALF)
    zeros = jnp.zeros((HALF, BLOCK), jnp.float32)
    square[:HALF] = mixed
    square[HALF:] = zeros
    turned = square[...].T
    square[:HALF] = zeros
    square[HALF:] = mixed
    above = square[...].T[:HALF]
    square[HALF:] = turned[:HALF]
    below = square[...].T[:HALF]
    r, c = iotas(HALF)
    top = jnp.where(r <= c, mixed, turned[:HALF])
    d = jnp.where(r > c - HALF, below, jnp.where(r < c - HALF, above, tail[3:4]))
    square[:HALF] = top
    square[HALF:] = jnp.where(c < HALF, turned[HALF:], d)
    found = [((0, 0), first), ((1, 1), second), ((2, 2), square[...])]
    return trace, found + [(at, get(i * BLOCK, BLOCK)) for i, at in enumerate(WHOLE, 1)]


def kernel(
    D, grads, counts, out,
    own, xin, packed, gath, done, gram_own, gram_out, gram_in, gram_all, square,
    load_sem, xin_send, xin_recv, z_send, z_recv, self_sem, back_send, back_recv, xout_send, xout_recv,
    gram_send, gram_recv,
):
    Z = D // 2
    span = Z // 4
    reach = 3 * Z // 8
    strip, cols = grads.shape[1], grads.shape[2]
    half = D // 2
    per_group = D // GROUPS
    per_part = D // PARTS
    per_chunk = D // 4
    me = lax.axis_index("dp")
    expert = lax.axis_index("expert")
    mate = expert + 1 - 2 * lax.rem(expert, 2)
    z, core = me // 2, lax.rem(me, 2)

    load = pltpu.make_async_copy(grads.at[pl.ds(0, D)], own, load_sem)
    load.start()

    barrier = pltpu.get_barrier_semaphore()

    @pl.loop(0, 2 * reach + 1)
    def _(k):
        far = lax.rem(z + Z + reach - k, Z) * 2

        @pl.loop(0, 2)
        def _(s):
            @pl.when(far + s != me)
            def _():
                pl.semaphore_signal(
                    barrier, inc=1, device_id=(far + s, expert), device_id_type=MESH
                )

    pl.semaphore_signal(barrier, inc=1, device_id=(me, mate), device_id_type=MESH)
    pl.semaphore_wait(barrier, 2 * (2 * reach + 1))

    def offset(role, m, s):
        return jnp.where(role == PRIMARY, reach - s - m, 1 - reach - s + m)

    def target_of(w, role, m):
        zt = z + offset(role, m, core) + 2 * Z
        slot = lax.rem(zt - role * span, Z) * 2 + w
        return slot, lax.rem(zt, Z) * 2 + w

    def outward(i):
        w, q = i // Z, lax.rem(i, Z)
        return w, lax.rem(q, 2), q // 2

    def turn_of(zj, w):
        return lax.rem(zj // span + w, 2)

    def homeward(i):
        turn, w, q = i // Z, lax.rem(i // (Z // 2), 2), lax.rem(i, Z // 2)
        zj = span * (2 * (q // span) + lax.rem(turn + w, 2)) + lax.rem(q, span)
        return 2 * zj + w

    def part_of(slot):
        zj, w = slot // 2, lax.rem(slot, 2)
        q = zj // (2 * span) * span + lax.rem(zj, span)
        return (turn_of(zj, w) * Z + w * (Z // 2) + q) // per_part

    def cross(g):
        @pl.loop(0, per_group)
        def _(k):
            j, _ = target_of(*outward(g * per_group + k))
            pltpu.make_async_remote_copy(
                src_ref=grads.at[2 * D - 1 - j],
                dst_ref=xin.at[j],
                send_sem=xin_send,
                recv_sem=xin_recv.at[g],
                device_id=(me, mate),
                device_id_type=MESH,
            ).start()

    cross(0)
    cross(1)

    load.wait()
    count = counts[0]

    @pl.loop(0, GROUPS)
    def _(g):
        @pl.when(g < GROUPS - 2)
        def _():
            cross(g + 2)

        pltpu.make_async_copy(
            xin.at[pl.ds(0, per_group)], xin.at[pl.ds(0, per_group)], xin_recv.at[g]
        ).wait()

        @pl.loop(0, per_group)
        def _(k):
            w, role, m = outward(g * per_group + k)
            j, target = target_of(w, role, m)
            packed[j] = jnp.where(j < count, own[j], xin[j])

            @pl.when(target != me)
            def _():
                pltpu.make_async_remote_copy(
                    src_ref=packed.at[j],
                    dst_ref=gath.at[role * half + 2 * m + core],
                    send_sem=z_send,
                    recv_sem=z_recv.at[2 * role + 2 * m // per_chunk],
                    device_id=(target, expert),
                    device_id_type=MESH,
                ).start()

            @pl.when(target == me)
            def _():
                gath[role * half + 2 * m + core] = packed[j]

    roles = [lax.rem(turn + turn_of(z, core), 2) for turn in (0, 1)]

    def exchange(turn):
        zt = lax.rem(z + jnp.where(roles[turn] == PRIMARY, span, Z - span), Z)
        return pltpu.make_async_remote_copy(
            src_ref=gram_out.at[turn],
            dst_ref=gram_in.at[turn],
            send_sem=gram_send.at[turn],
            recv_sem=gram_recv.at[turn],
            device_id=(zt * 2 + core, expert),
            device_id_type=MESH,
        )

    def rows_of(role, c):
        start = role * half + c * per_chunk
        return gath[pl.ds(start, per_chunk)].reshape(per_chunk * strip, cols)

    rows_i = lax.broadcasted_iota(jnp.int32, (cols, cols), 0)
    cols_i = lax.broadcasted_iota(jnp.int32, (cols, cols), 1)
    traces = []
    for turn, role in enumerate(roles):
        gram = jnp.zeros((cols, cols), jnp.float32)
        for c in range(2):
            n = per_chunk - c
            pltpu.make_async_copy(
                gath.at[pl.ds(0, n)], gath.at[pl.ds(0, n)], z_recv.at[2 * role + c]
            ).wait()
            gram = gram + transposed_dot(rows_of(role, c))
        gram_own[turn] = gram
        trace = jnp.sum(jnp.where(rows_i == cols_i, gram, 0.0), keepdims=True)

        def put(start, n, values, turn=turn):
            gram_out[turn, start : start + n] = values.astype(jnp.bfloat16)

        pack(gram, trace, square, put)
        traces.append(trace)
        exchange(turn).start()

    def slot_in(role):
        return lax.rem(z + Z - role * span, Z) * 2 + core

    def back(role, m, s):
        zs = lax.rem(z - offset(role, m, s) + 2 * Z, Z)
        return zs, pltpu.make_async_remote_copy(
            src_ref=done.at[role * half + 2 * m + s],
            dst_ref=out.at[slot_in(role)],
            send_sem=back_send,
            recv_sem=back_recv.at[part_of(slot_in(role))],
            device_id=(zs * 2 + s, expert),
            device_id_type=MESH,
        )

    def keep(turn):
        role = roles[turn]
        m = jnp.where(role == PRIMARY, reach - core, reach - 1 + core)
        return pltpu.make_async_copy(
            done.at[role * half + 2 * m + core], out.at[slot_in(role)], self_sem.at[turn]
        )

    scale_out = math.sqrt(D * strip)
    for turn, role in enumerate(roles):
        exchange(turn).wait_recv()

        def get(start, n, turn=turn):
            return gram_in[turn, start : start + n].astype(jnp.float32)

        trace, others = unpack(square, get)
        inv = 1.0 / (jnp.sqrt(traces[turn] + trace) + 1e-07)
        for (a, b), other in others:
            whole = (gram_own[(turn, *block(a, b))] + other) * inv * inv
            gram_all[block(a, b)] = whole.astype(jnp.bfloat16)
            if a != b:
                gram_all[block(b, a)] = whole.T.astype(jnp.bfloat16)
        gram = gram_all[...]
        poly = polynomial(gram)
        next_poly = polynomial(gram_after(gram, poly))
        for c in range(2):
            part = (rows_of(role, c).astype(jnp.float32) * inv).astype(jnp.bfloat16)
            part = (poly_first * part.astype(jnp.float32) + dot(part, poly)).astype(jnp.bfloat16)
            updated = poly_first * part.astype(jnp.float32) + dot(part, next_poly)
            start = role * half + c * per_chunk
            done[pl.ds(start, per_chunk)] = (
                (updated * scale_out).astype(jnp.bfloat16).reshape(per_chunk, strip, cols)
            )

        @pl.loop(0, (len(LATER) + 1) * half)
        def _(i):
            s = lax.rem(i, 2)
            zs, copy = back(role, lax.rem(i // 2, Z // 2), s)
            rank = sum((zs >= Z * n // 32).astype(jnp.int32) for n in LATER)

            @pl.when(jnp.logical_and(zs * 2 + s != me, rank == i // half))
            def _():
                copy.start()

        keep(turn).start()

    keep(0).wait()
    keep(1).wait()

    own_parts = [part_of(slot_in(role)) for role in roles]

    @pl.loop(0, PARTS)
    def _(g):
        kept = (g == own_parts[0]).astype(jnp.int32) + (g == own_parts[1]).astype(jnp.int32)

        def arrived(n):
            if n:
                pltpu.make_async_copy(
                    xin.at[pl.ds(0, n)], xin.at[pl.ds(0, n)], back_recv.at[g]
                ).wait()

        @pl.when(kept == 1)
        def _():
            arrived(per_part - 1)

        @pl.when(kept == 0)
        def _():
            arrived(per_part)

        @pl.loop(0, per_part)
        def _(k):
            j = homeward(g * per_part + k)
            pltpu.make_async_remote_copy(
                src_ref=out.at[j],
                dst_ref=out.at[2 * D - 1 - j],
                send_sem=xout_send,
                recv_sem=xout_recv,
                device_id=(me, mate),
                device_id_type=MESH,
            ).start()

    def wait_all(ref, sem):
        pltpu.make_async_copy(ref, ref, sem).wait()

    wait_all(xin, xin_send)
    wait_all(packed.at[pl.ds(0, D - 2)], z_send)
    exchange(0).wait_send()
    exchange(1).wait_send()
    wait_all(done.at[pl.ds(0, D - 2)], back_send)
    wait_all(out.at[pl.ds(0, D)], xout_send)
    wait_all(out.at[pl.ds(0, D)], xout_recv)


def body(D, grads, counts):
    held = grads[0]
    slots, strip, cols = held.shape
    bf16 = functools.partial(pltpu.VMEM, dtype=jnp.bfloat16)
    dma = pltpu.SemaphoreType.DMA
    moved = pl.pallas_call(
        functools.partial(kernel, D),
        out_shape=jax.ShapeDtypeStruct((slots, strip, cols), jnp.bfloat16),
        in_specs=[pl.BlockSpec(memory_space=pltpu.HBM), pl.BlockSpec(memory_space=pltpu.SMEM)],
        out_specs=pl.BlockSpec(memory_space=pl.ANY),
        scratch_shapes=[
            bf16((D, strip, cols)),
            bf16((D, strip, cols)),
            bf16((D, strip, cols)),
            bf16((D, strip, cols)),
            bf16((D, strip, cols)),
            pltpu.VMEM((2, cols, cols), jnp.float32),
            bf16((2, GRAM_ROWS, BLOCK)),
            bf16((2, GRAM_ROWS, BLOCK)),
            bf16((cols, cols)),
            pltpu.VMEM((BLOCK, BLOCK), jnp.float32),
            dma,
            dma,
            dma((GROUPS,)),
            dma,
            dma((4,)),
            dma((2,)),
            dma,
            dma((PARTS,)),
            dma,
            dma,
            dma((2,)),
            dma((2,)),
        ],
        compiler_params=pltpu.CompilerParams(
            collective_id=0, has_side_effects=True, vmem_limit_bytes=62 * 1024 * 1024
        ),
    )(held, counts)
    slot_ids = jnp.arange(slots, dtype=jnp.int32)
    result = jnp.where((slot_ids < counts[0])[:, None, None], moved, jnp.zeros_like(moved))
    return result[None]


def solution(mesh):
    placed = (P("expert", None, "dp", None), P("expert"))
    return jax.shard_map(
        functools.partial(body, mesh.shape["dp"]),
        mesh=mesh,
        in_specs=placed,
        out_specs=P("expert", None, "dp", None),
        check_vma=False,
    )
```
